32 devices in a mesh: leaf: 4 (over y, x), owner: 8 (over z, core).
Axes of the slice: x: 2, y: 2, z: 4, core: 2. Of those that a mesh axis runs over, the one named last changes fastest.
Arguments:
- multipoles: float32 [3, 343, 12288], P(None, None, ('leaf', 'owner')), may hold values from -6 to 6
- operators: bfloat16 [4, 1029, 1029], replicated, may hold values from -0.1875 to 0.1875
- lists: int32 [12288, 4], P(('leaf', 'owner')), may hold values from -1 to 447, as said below
- send_slots: int32 [32, 8, 4], P(('leaf', 'owner')), may hold values from -1 to 31, as said below
Outputs:
- locals_out: float32 [3, 343, 12288], P(None, None, ('leaf', 'owner'))
The draws below stay inside these ranges and needn't reach their ends.
Inputs may be any that keep to these rules, and one draw needn't show every extreme that they name: `lists`: A code of the first kind appears only for boxes of groups other than the first, of the third kind only for groups other than the last; a code naming (p, c) appears only where send_slots of owner p for this owner holds a slot at c, and never with p equal to the box's own owner. `send_slots`: entries are distinct boundary slots followed by -1 padding; the entries for an owner itself are all -1; every draw fills some pair's 4 entries.
All inputs are finite; a program needn't handle non-finite values.
Results may differ from the reference program's by a relative error of at most 0.0029.
Values may be sent and summed in bfloat16 or wider, within the bound.
A program may use at most 128 MiB of HBM per device.

```python
import jax
import jax.numpy as jnp

COMP = 3
NODES = 343
DIRS = 4
BOX_DEV = 384
FACE = 16
BOUND = 32
CAP = 4
GROUPS = 4
OWNERS = 8
DEVS = 32
BOXES = 12288


def joint_tables(key):
    base = jax.random.fold_in(key, 31)
    keys = jax.random.split(base, 11)
    scores = jax.random.randint(keys[0], (DEVS, OWNERS, BOUND), 0, BOUND) * BOUND + jnp.arange(BOUND, dtype=jnp.int32)
    order = jnp.argsort(scores, axis=-1)[:, :, :CAP].astype(jnp.int32)
    sender = jnp.arange(DEVS, dtype=jnp.int32)[:, None]
    peer = jnp.arange(OWNERS, dtype=jnp.int32)[None, :]
    receiver = sender // OWNERS * OWNERS + peer
    hotness = jax.random.randint(keys[1], (DEVS,), 0, CAP + 1)
    drawn = jax.random.randint(keys[2], (DEVS, OWNERS), 0, CAP + 1)
    count = jnp.minimum(CAP, drawn + hotness[receiver])
    chosen_sender = jax.random.randint(keys[3], (), 0, DEVS)
    chosen_peer = (chosen_sender % OWNERS + 1 + jax.random.randint(keys[4], (), 0, OWNERS - 1)) % OWNERS
    forced = (sender == chosen_sender) & (peer == chosen_peer)
    count = jnp.where(forced, CAP, count)
    count = jnp.where(peer == sender % OWNERS, 0, count)
    places = jnp.arange(CAP, dtype=jnp.int32)[None, None, :]
    provided = jnp.where(places < count[:, :, None], order, -1).astype(jnp.int32)
    shape = (DEVS, BOX_DEV, DIRS)
    device = jnp.arange(DEVS, dtype=jnp.int32)[:, None, None]
    group = device // OWNERS
    mine = jnp.broadcast_to(device % OWNERS, shape)
    kind = jax.random.randint(keys[5], shape, 0, 20)
    local_code = FACE + jax.random.randint(keys[6], shape, 0, BOX_DEV)
    side_low = jax.random.randint(keys[7], shape, 0, 2) == 0
    rim = jax.random.randint(keys[8], shape, 0, FACE)
    halo_code = jnp.where(side_low, rim, FACE + BOX_DEV + rim)
    halo_ok = jnp.where(side_low, group > 0, group < GROUPS - 1)
    other = jax.random.randint(keys[9], shape, 0, OWNERS)
    column = jax.random.randint(keys[10], shape, 0, CAP)
    source_dev = group * OWNERS + other
    slot = provided[source_dev, mine, column]
    ghost_code = 2 * FACE + BOX_DEV + other * CAP + column
    code = local_code
    code = jnp.where((kind >= 10) & (kind < 13) & halo_ok, halo_code, code)
    code = jnp.where((kind >= 13) & (slot >= 0), ghost_code, code)
    code = jnp.where(kind < 3, -1, code)
    return (provided, code.reshape(DEVS * BOX_DEV, DIRS).astype(jnp.int32))


def draw_lists(key, part):
    return joint_tables(key)[1]


def draw_send_slots(key, part):
    return joint_tables(key)[0]


def block_levels(stream_key, shape, cuts, low, largest):
    factor_of = 1.0
    for dim, blocks in cuts:
        steps = jax.random.uniform(jax.random.fold_in(jax.random.fold_in(stream_key, 6), dim), (blocks,), jnp.float32, low / len(cuts), largest / len(cuts))
        factor_of = factor_of * jnp.repeat(jnp.exp(steps), shape[dim] // blocks).reshape((-1,) + (1,) * (len(shape) - 1 - dim))
    return factor_of


def bell_draw(key, extent, scale, most, pieces=(), held_as=jnp.bfloat16):
    drawn = scale * jax.random.normal(key, extent, jnp.float32)
    if pieces:
        drawn = drawn * block_levels(key, extent, pieces, -0.22, 0.18)
    return jnp.clip(drawn, -most, most).astype(held_as)


def setup_inputs(seed: int = 0) -> dict:
    streams_of = jax.random.split(jax.random.key(seed), 5)
    multipoles = bell_draw(streams_of[0], (COMP, NODES, BOXES), 1.0, 6.0, ((2, 32),), jnp.float32)
    operators = bell_draw(streams_of[1], (DIRS, COMP * NODES, COMP * NODES), (COMP * NODES) ** -0.5, 0.1875)
    lists = draw_lists(jax.random.fold_in(streams_of[4], 71), 0)
    send_slots = draw_send_slots(jax.random.fold_in(streams_of[4], 71), 0)
    return {"multipoles": multipoles, "operators": operators, "lists": lists, "send_slots": send_slots}


def reference(multipoles, operators, lists, send_slots):
    width = COMP * NODES
    packed = multipoles.reshape(width, BOXES).astype(jnp.bfloat16)
    rows = jnp.arange(BOXES, dtype=jnp.int32)[:, None]
    device = rows // BOX_DEV
    group = device // OWNERS
    mine = device % OWNERS
    code = lists
    lower = (device - OWNERS) * BOX_DEV + BOX_DEV - FACE + code
    here = device * BOX_DEV + code - FACE
    upper = (device + OWNERS) * BOX_DEV + code - FACE - BOX_DEV
    ghost = jnp.maximum(code - 2 * FACE - BOX_DEV, 0)
    peer = ghost // CAP
    column = ghost % CAP
    provider = group * OWNERS + peer
    slot = send_slots[jnp.clip(provider, 0, DEVS - 1), jnp.broadcast_to(mine, code.shape), column]
    remote = provider * BOX_DEV + jnp.maximum(slot, 0)
    target = jnp.where(code < FACE, lower, jnp.where(code < FACE + BOX_DEV, here, jnp.where(code < 2 * FACE + BOX_DEV, upper, remote)))
    valid = code >= 0
    valid = valid & jnp.where(code < FACE, group > 0, True)
    valid = valid & jnp.where((code >= FACE + BOX_DEV) & (code < 2 * FACE + BOX_DEV), group < GROUPS - 1, True)
    target = jnp.where(valid, target, 0).astype(jnp.int32)
    total = jnp.zeros((width, BOXES), jnp.float32)
    for direction in range(DIRS):
        present = valid[:, direction].astype(jnp.bfloat16)
        columns = jnp.take(packed, target[:, direction], axis=1) * present[None, :]
        total = total + jnp.dot(operators[direction], columns, preferred_element_type=jnp.float32)
    return total.reshape(COMP, NODES, BOXES)
```

```python
import functools

import jax
import jax.numpy as jnp
from jax import lax
from jax.experimental import pallas as pl
from jax.experimental.pallas import tpu as pltpu
from jax.sharding import PartitionSpec as P

FACE = 16
BOUND = 32
LANES = 128
F32 = jnp.float32
BF16 = jnp.bfloat16
MESH = pl.DeviceIdType.MESH


def round_up(value, unit):
    return (value + unit - 1) // unit * unit


def iota(shape, dim):
    return lax.broadcasted_iota(jnp.int32, shape, dim)


def one_hot(condition):
    return jnp.where(condition, 1.0, 0.0).astype(BF16)


def dot_nt(a, b):
    return lax.dot_general(a, b, (((1,), (1,)), ((), ())), preferred_element_type=F32)


def kernel(
    groups, owners, cap, first,
    mult, ops, lists, slots, out,
    opv, mv, packf, packed, pb, y_first, y_rest, ga, gb, face_out, face_in, ghost_out, ghost_in,
    op_sem, m_sem, face_send, face_recv, ghost_send, ghost_recv,
):
    comps, nodes, nboxes = mv.shape
    width = comps * nodes
    dirs = lists.shape[0]
    rest = nboxes - first
    span = y_first.shape[1] // dirs
    leaf = lax.axis_index("leaf")
    me = lax.axis_index("owner")

    def op_copy(c):
        rows = pl.ds(c * nodes, nodes)
        return pltpu.make_async_copy(ops.at[rows], opv.at[c, pl.ds(0, nodes)], op_sem.at[c])

    m_copy = pltpu.make_async_copy(mult, mv, m_sem)
    m_copy.start()
    for c in range(comps):
        op_copy(c).start()

    face_in[...] = jnp.zeros_like(face_in)
    ghost_in[...] = jnp.zeros_like(ghost_in)

    barrier = pltpu.get_barrier_semaphore()

    def greet(k, carry):
        peer = lax.rem(me + k, owners)
        pl.semaphore_signal(barrier, inc=1, device_id=(leaf, peer), device_id_type=MESH)
        return carry

    lax.fori_loop(1, owners, greet, 0)

    @pl.when(leaf > 0)
    def _():
        pl.semaphore_signal(barrier, inc=1, device_id=(leaf - 1, me), device_id_type=MESH)

    @pl.when(leaf < groups - 1)
    def _():
        pl.semaphore_signal(barrier, inc=1, device_id=(leaf + 1, me), device_id_type=MESH)

    rows = owners * cap
    spread = jnp.where(iota((rows, owners), 0) // cap == iota((rows, owners), 1), 1.0, 0.0)
    spread = dot_nt(spread.astype(BF16), slots[...].astype(F32).astype(BF16))
    here = iota((rows, cap), 0) % cap == iota((rows, cap), 1)
    slot = jnp.sum(jnp.where(here, spread, 0.0), axis=1, keepdims=True)
    chooser = one_hot(iota((rows, LANES), 1).astype(F32) == slot)
    low_pick = one_hot(iota((FACE, LANES), 0) == iota((FACE, LANES), 1))
    high_pick = one_hot(iota((FACE, LANES), 0) + (LANES - FACE) == iota((FACE, LANES), 1))

    m_copy.wait()
    for c in range(comps):
        packf[pl.ds(c * nodes, nodes), :] = mv[c]
    packed[...] = packf[...].astype(BF16)
    head = packed[:, :LANES]
    tail = packed[:, nboxes - LANES:]
    picked = dot_nt(jnp.concatenate([low_pick, chooser], axis=0), head)
    face_out[0] = picked[:FACE].astype(BF16)
    face_out[1] = dot_nt(high_pick, tail).astype(BF16)
    for p in range(owners):
        ghost_out[p] = picked[FACE + p * cap:FACE + (p + 1) * cap].astype(BF16)

    barrier_count = owners - 1 + jnp.where(leaf > 0, 1, 0) + jnp.where(leaf < groups - 1, 1, 0)
    pl.semaphore_wait(barrier, barrier_count)

    def face_copy(side):
        step = -1 if side == 0 else 1
        return pltpu.make_async_remote_copy(
            src_ref=face_out.at[side], dst_ref=face_in.at[1 - side],
            send_sem=face_send.at[side], recv_sem=face_recv.at[1 - side],
            device_id=(leaf + step, me), device_id_type=MESH,
        )

    def ghost_copy(k):
        peer = lax.rem(me + k, owners)
        return pltpu.make_async_remote_copy(
            src_ref=ghost_out.at[peer], dst_ref=ghost_in.at[me],
            send_sem=ghost_send.at[k], recv_sem=ghost_recv.at[k],
            device_id=(leaf, peer), device_id_type=MESH,
        )

    @pl.when(leaf > 0)
    def _():
        face_copy(0).start()

    @pl.when(leaf < groups - 1)
    def _():
        face_copy(1).start()

    lax.fori_loop(1, owners, lambda k, carry: (ghost_copy(k).start(), carry)[1], 0)

    code = lists[...]
    place = jnp.where(
        code < 0, -1,
        jnp.where(code < FACE, code + nboxes, jnp.where(code < FACE + nboxes, code - FACE, code)),
    )
    for d in range(dirs):
        row = place[d:d + 1, :]
        ga[d] = one_hot(iota((first, nboxes), 0) == row)
        gb[d] = one_hot(iota((gb.shape[1], nboxes), 0) + first == row)

    def translate(c, weights, select):
        lhs = opv[c].reshape(span * dirs, width)
        y = y_first if weights.shape[1] == first else y_rest
        product = jnp.dot(lhs, weights, preferred_element_type=F32)
        for t in range(y.shape[0]):
            y[t] = product[:, t * LANES:(t + 1) * LANES]
        total = None
        for d in range(dirs):
            part = jnp.concatenate(
                [y[t, pl.ds(d, span, stride=dirs), :].astype(BF16) for t in range(y.shape[0])],
                axis=1,
            )
            term = jnp.dot(part, select[d], preferred_element_type=F32)
            total = term if total is None else total + term
        return total[:nodes]

    def first_pass(c, carry):
        op_copy(c).wait()
        out[c] = translate(c, packed[:, :first], ga)
        return carry

    lax.fori_loop(0, comps, first_pass, 0)

    @pl.when(leaf < groups - 1)
    def _():
        face_copy(1).wait_send()
        face_copy(0).wait_recv()

    @pl.when(leaf > 0)
    def _():
        face_copy(0).wait_send()
        face_copy(1).wait_recv()

    lax.fori_loop(1, owners, lambda k, carry: (ghost_copy(k).wait(), carry)[1], 0)

    pieces = [face_in[0].astype(F32), face_in[1].astype(F32)]
    ghosts = [ghost_in[p].astype(F32) for p in range(owners)]
    table = jnp.concatenate(pieces + ghosts, axis=0)
    pad = gb.shape[1] - rest - table.shape[0]
    if pad:
        table = jnp.concatenate([table, jnp.zeros((pad, width), F32)], axis=0)
    pb[:, :rest] = packed[:, first:]
    pb[:, rest:] = table.T.astype(BF16)

    def second_pass(c, carry):
        out[c] = out[c] + translate(c, pb[...], gb)
        return carry

    lax.fori_loop(0, comps, second_pass, 0)


def local(groups, owners, multipoles, operators, lists, send_slots):
    comps, nodes, nboxes = multipoles.shape
    dirs, width, _ = operators.shape
    cap = send_slots.shape[2]
    first = nboxes // 256 * 256 if nboxes % 256 else nboxes - 256
    extra = round_up(nboxes - first + 2 * FACE + owners * cap, LANES)
    extra = max(extra, 256)
    span = round_up(nodes, 8)
    anywhere = pl.BlockSpec(memory_space=pl.ANY)
    vmem = pl.BlockSpec(memory_space=pltpu.VMEM)
    dma = pltpu.SemaphoreType.DMA
    return pl.pallas_call(
        functools.partial(kernel, groups, owners, cap, first),
        out_shape=jax.ShapeDtypeStruct((comps, nodes, nboxes), F32),
        in_specs=[anywhere, anywhere, vmem, vmem],
        out_specs=vmem,
        scratch_shapes=[
            pltpu.VMEM((comps, span, dirs, width), BF16),
            pltpu.VMEM((comps, nodes, nboxes), F32),
            pltpu.VMEM((width, nboxes), F32),
            pltpu.VMEM((width, nboxes), BF16),
            pltpu.VMEM((width, extra), BF16),
            pltpu.VMEM((first // LANES, span * dirs, LANES), F32),
            pltpu.VMEM((extra // LANES, span * dirs, LANES), F32),
            pltpu.VMEM((dirs, first, nboxes), BF16),
            pltpu.VMEM((dirs, extra, nboxes), BF16),
            pltpu.VMEM((2, FACE, width), BF16),
            pltpu.VMEM((2, FACE, width), BF16),
            pltpu.VMEM((owners, cap, width), BF16),
            pltpu.VMEM((owners, cap, width), BF16),
            dma((comps,)), dma, dma((2,)), dma((2,)), dma((owners,)), dma((owners,)),
        ],
        compiler_params=pltpu.CompilerParams(
            collective_id=0, has_side_effects=True, vmem_limit_bytes=58 << 20
        ),
        cost_estimate=pl.CostEstimate(
            flops=2 * dirs * width * width * nboxes,
            bytes_accessed=2 * dirs * width * width + 8 * width * nboxes,
            transcendentals=0,
        ),
    )(
        multipoles,
        operators.transpose(1, 0, 2),
        lists.T,
        send_slots.reshape(owners, cap).T,
    )


def solution(mesh):
    return jax.shard_map(
        functools.partial(local, mesh.shape["leaf"], mesh.shape["owner"]),
        mesh=mesh,
        in_specs=(
            P(None, None, ("leaf", "owner")),
            P(),
            P(("leaf", "owner"), None),
            P(("leaf", "owner"), None, None),
        ),
        out_specs=P(None, None, ("leaf", "owner")),
        check_vma=False,
    )
```

```python
import functools

import jax
import jax.numpy as jnp
from jax import lax
from jax.experimental import pallas as pl
from jax.experimental.pallas import tpu as pltpu
from jax.sharding import PartitionSpec as P

FACE = 16
BOUND = 32
LANES = 128
F32 = jnp.float32
BF16 = jnp.bfloat16
MESH = pl.DeviceIdType.MESH


def round_up(value, unit):
    return (value + unit - 1) // unit * unit


def iota(shape, dim):
    return lax.broadcasted_iota(jnp.int32, shape, dim)


def one_hot(condition):
    return jnp.where(condition, 1.0, 0.0).astype(BF16)


def dot_nt(a, b):
    return lax.dot_general(a, b, (((1,), (1,)), ((), ())), preferred_element_type=F32)


def kernel(
    groups, owners, cap, first,
    mult, ops, lists, slots, out,
    opv, mv, packf, packed, pb, y_first, y_rest, z, g, face_out, face_in, ghost_out, ghost_in,
    op_sem, m_sem, face_send, face_recv, ghost_send, ghost_recv,
):
    comps, nodes, nboxes = mv.shape
    width = comps * nodes
    dirs = lists.shape[0]
    rest = nboxes - first
    span = y_first.shape[1] // dirs
    table = g.shape[0] // dirs
    leaf = lax.axis_index("leaf")
    me = lax.axis_index("owner")

    def op_copy(c):
        rows = pl.ds(c * nodes, nodes)
        return pltpu.make_async_copy(ops.at[rows], opv.at[c, pl.ds(0, nodes)], op_sem.at[c])

    m_copy = pltpu.make_async_copy(mult, mv, m_sem)
    m_copy.start()
    for c in range(comps):
        op_copy(c).start()

    face_in[...] = jnp.zeros_like(face_in)
    ghost_in[...] = jnp.zeros_like(ghost_in)

    barrier = pltpu.get_barrier_semaphore()

    def greet(k, carry):
        peer = lax.rem(me + k, owners)
        pl.semaphore_signal(barrier, inc=1, device_id=(leaf, peer), device_id_type=MESH)
        return carry

    lax.fori_loop(1, owners, greet, 0)

    @pl.when(leaf > 0)
    def _():
        pl.semaphore_signal(barrier, inc=1, device_id=(leaf - 1, me), device_id_type=MESH)

    @pl.when(leaf < groups - 1)
    def _():
        pl.semaphore_signal(barrier, inc=1, device_id=(leaf + 1, me), device_id_type=MESH)

    rows = owners * cap
    spread = jnp.where(iota((rows, owners), 0) // cap == iota((rows, owners), 1), 1.0, 0.0)
    spread = dot_nt(spread.astype(BF16), slots[...].astype(F32).astype(BF16))
    here = iota((rows, cap), 0) % cap == iota((rows, cap), 1)
    slot = jnp.sum(jnp.where(here, spread, 0.0), axis=1, keepdims=True)
    chooser = one_hot(iota((rows, LANES), 1).astype(F32) == slot)
    low_pick = one_hot(iota((FACE, LANES), 0) == iota((FACE, LANES), 1))
    high_pick = one_hot(iota((FACE, LANES), 0) + (LANES - FACE) == iota((FACE, LANES), 1))

    code = lists[...]
    place = jnp.where(
        code < 0, -1,
        jnp.where(code < FACE, code + nboxes, jnp.where(code < FACE + nboxes, code - FACE, code)),
    )
    for d in range(dirs):
        g[d * table:(d + 1) * table] = one_hot(iota((table, nboxes), 0) == place[d:d + 1, :])

    m_copy.wait()
    for c in range(comps):
        packf[pl.ds(c * nodes, nodes), :] = mv[c]
    packed[...] = packf[...].astype(BF16)
    head = packed[:, :LANES]
    tail = packed[:, nboxes - LANES:]
    picked = dot_nt(jnp.concatenate([low_pick, chooser], axis=0), head)
    face_out[0] = picked[:FACE].astype(BF16)
    face_out[1] = dot_nt(high_pick, tail).astype(BF16)
    for p in range(owners):
        ghost_out[p] = picked[FACE + p * cap:FACE + (p + 1) * cap].astype(BF16)

    barrier_count = owners - 1 + jnp.where(leaf > 0, 1, 0) + jnp.where(leaf < groups - 1, 1, 0)
    pl.semaphore_wait(barrier, barrier_count)

    def face_copy(side):
        step = -1 if side == 0 else 1
        return pltpu.make_async_remote_copy(
            src_ref=face_out.at[side], dst_ref=face_in.at[1 - side],
            send_sem=face_send.at[side], recv_sem=face_recv.at[1 - side],
            device_id=(leaf + step, me), device_id_type=MESH,
        )

    def ghost_copy(k):
        peer = lax.rem(me + k, owners)
        return pltpu.make_async_remote_copy(
            src_ref=ghost_out.at[peer], dst_ref=ghost_in.at[me],
            send_sem=ghost_send.at[k], recv_sem=ghost_recv.at[k],
            device_id=(leaf, peer), device_id_type=MESH,
        )

    @pl.when(leaf > 0)
    def _():
        face_copy(0).start()

    @pl.when(leaf < groups - 1)
    def _():
        face_copy(1).start()

    lax.fori_loop(1, owners, lambda k, carry: (ghost_copy(k).start(), carry)[1], 0)

    def translate(c, weights, y, start):
        lhs = opv[c].reshape(span * dirs, width)
        product = jnp.dot(lhs, weights, preferred_element_type=F32)
        for t in range(y.shape[0]):
            y[t] = product[:, t * LANES:(t + 1) * LANES]
        for d in range(dirs):
            for t in range(y.shape[0]):
                at = d * table + start + t * LANES
                z[c, :span, at:at + LANES] = y[t, pl.ds(d, span, stride=dirs), :].astype(BF16)

    def first_pass(c, carry):
        op_copy(c).wait()
        translate(c, packed[:, :first], y_first, 0)
        return carry

    lax.fori_loop(0, comps, first_pass, 0)

    @pl.when(leaf < groups - 1)
    def _():
        face_copy(1).wait_send()
        face_copy(0).wait_recv()

    @pl.when(leaf > 0)
    def _():
        face_copy(0).wait_send()
        face_copy(1).wait_recv()

    lax.fori_loop(1, owners, lambda k, carry: (ghost_copy(k).wait(), carry)[1], 0)

    arrived = [face_in[0].astype(F32), face_in[1].astype(F32)]
    ghosts = [ghost_in[p].astype(F32) for p in range(owners)]
    arrived = jnp.concatenate(arrived + ghosts, axis=0)
    pad = pb.shape[1] - rest - arrived.shape[0]
    if pad:
        arrived = jnp.concatenate([arrived, jnp.zeros((pad, width), F32)], axis=0)
    pb[:, :rest] = packed[:, first:]
    pb[:, rest:] = arrived.T.astype(BF16)

    def second_pass(c, carry):
        translate(c, pb[...], y_rest, first)
        return carry

    lax.fori_loop(0, comps, second_pass, 0)

    held = z.shape[1]
    result = jnp.dot(z[...].reshape(comps * held, dirs * table), g[...], preferred_element_type=F32)
    for c in range(comps):
        out[c] = result[c * held:c * held + nodes]


def local(groups, owners, multipoles, operators, lists, send_slots):
    comps, nodes, nboxes = multipoles.shape
    dirs, width, _ = operators.shape
    cap = send_slots.shape[2]
    first = nboxes // 256 * 256 if nboxes % 256 else nboxes - 256
    extra = round_up(nboxes - first + 2 * FACE + owners * cap, LANES)
    extra = max(extra, 256)
    span = round_up(nodes, 8)
    anywhere = pl.BlockSpec(memory_space=pl.ANY)
    vmem = pl.BlockSpec(memory_space=pltpu.VMEM)
    dma = pltpu.SemaphoreType.DMA
    return pl.pallas_call(
        functools.partial(kernel, groups, owners, cap, first),
        out_shape=pltpu.VMEM((comps, nodes, nboxes), F32),
        in_specs=[anywhere, anywhere, vmem, vmem],
        out_specs=vmem,
        scratch_shapes=[
            pltpu.VMEM((comps, span, dirs, width), BF16),
            pltpu.VMEM((comps, nodes, nboxes), F32),
            pltpu.VMEM((width, nboxes), F32),
            pltpu.VMEM((width, nboxes), BF16),
            pltpu.VMEM((width, extra), BF16),
            pltpu.VMEM((first // LANES, span * dirs, LANES), F32),
            pltpu.VMEM((extra // LANES, span * dirs, LANES), F32),
            pltpu.VMEM((comps, round_up(nodes, 16), dirs * (first + extra)), BF16),
            pltpu.VMEM((dirs * (first + extra), nboxes), BF16),
            pltpu.VMEM((2, FACE, width), BF16),
            pltpu.VMEM((2, FACE, width), BF16),
            pltpu.VMEM((owners, cap, width), BF16),
            pltpu.VMEM((owners, cap, width), BF16),
            dma((comps,)), dma, dma((2,)), dma((2,)), dma((owners,)), dma((owners,)),
        ],
        compiler_params=pltpu.CompilerParams(
            collective_id=0, has_side_effects=True, vmem_limit_bytes=58 << 20
        ),
        cost_estimate=pl.CostEstimate(
            flops=2 * dirs * width * width * nboxes,
            bytes_accessed=2 * dirs * width * width + 8 * width * nboxes,
            transcendentals=0,
        ),
    )(
        multipoles,
        operators.transpose(1, 0, 2),
        lists.T,
        send_slots.reshape(owners, cap).T,
    )


def solution(mesh):
    return jax.shard_map(
        functools.partial(local, mesh.shape["leaf"], mesh.shape["owner"]),
        mesh=mesh,
        in_specs=(
            P(None, None, ("leaf", "owner")),
            P(),
            P(("leaf", "owner"), None),
            P(("leaf", "owner"), None, None),
        ),
        out_specs=P(None, None, ("leaf", "owner")),
        check_vma=False,
    )
```

```python
import functools

import jax
import jax.numpy as jnp
from jax import lax
from jax.experimental import pallas as pl
from jax.experimental.pallas import tpu as pltpu
from jax.sharding import PartitionSpec as P

FACE = 16
BOUND = 32
LANES = 128
F32 = jnp.float32
BF16 = jnp.bfloat16
MESH = pl.DeviceIdType.MESH


def round_up(value, unit):
    return (value + unit - 1) // unit * unit


def iota(shape, dim):
    return lax.broadcasted_iota(jnp.int32, shape, dim)


def one_hot(condition):
    return jnp.where(condition, 1.0, 0.0).astype(BF16)


def dot_nt(a, b):
    return lax.dot_general(a, b, (((1,), (1,)), ((), ())), preferred_element_type=F32)


def kernel(
    groups, owners, cap, first,
    mult, ops, lists, slots, out,
    opv, mv, packf, packed, pb, y_first, y_rest, za, zb, ga, gb, face_out, face_in, ghost_out, ghost_in,
    op_sem, m_sem, face_send, face_recv, ghost_send, ghost_recv,
):
    comps, nodes, nboxes = mv.shape
    width = comps * nodes
    dirs = lists.shape[0]
    rest = nboxes - first
    span = y_first.shape[1] // dirs
    extra = pb.shape[1]
    leaf = lax.axis_index("leaf")
    me = lax.axis_index("owner")

    def op_copy(c):
        rows = pl.ds(c * nodes, nodes)
        return pltpu.make_async_copy(ops.at[rows], opv.at[c, pl.ds(0, nodes)], op_sem.at[c])

    m_copy = pltpu.make_async_copy(mult, mv, m_sem)
    m_copy.start()
    op_copy(0).start()

    face_in[...] = jnp.zeros_like(face_in)
    ghost_in[...] = jnp.zeros_like(ghost_in)

    barrier = pltpu.get_barrier_semaphore()

    def greet(k, carry):
        peer = lax.rem(me + k, owners)
        pl.semaphore_signal(barrier, inc=1, device_id=(leaf, peer), device_id_type=MESH)
        return carry

    lax.fori_loop(1, owners, greet, 0)

    @pl.when(leaf > 0)
    def _():
        pl.semaphore_signal(barrier, inc=1, device_id=(leaf - 1, me), device_id_type=MESH)

    @pl.when(leaf < groups - 1)
    def _():
        pl.semaphore_signal(barrier, inc=1, device_id=(leaf + 1, me), device_id_type=MESH)

    rows = owners * cap
    spread = jnp.where(iota((rows, owners), 0) // cap == iota((rows, owners), 1), 1.0, 0.0)
    spread = dot_nt(spread.astype(BF16), slots[...].astype(F32).astype(BF16))
    here = iota((rows, cap), 0) % cap == iota((rows, cap), 1)
    slot = jnp.sum(jnp.where(here, spread, 0.0), axis=1, keepdims=True)
    chooser = one_hot(iota((rows, LANES), 1).astype(F32) == slot)
    low_pick = one_hot(iota((FACE, LANES), 0) == iota((FACE, LANES), 1))
    high_pick = one_hot(iota((FACE, LANES), 0) + (LANES - FACE) == iota((FACE, LANES), 1))

    code = lists[...]
    place = jnp.where(
        code < 0, -1,
        jnp.where(code < FACE, code + nboxes, jnp.where(code < FACE + nboxes, code - FACE, code)),
    )
    for d in range(dirs):
        row = place[d:d + 1, :]
        ga[d * first:(d + 1) * first] = one_hot(iota((first, nboxes), 0) == row)
        gb[d * extra:(d + 1) * extra] = one_hot(iota((extra, nboxes), 0) + first == row)

    m_copy.wait()
    for c in range(1, comps):
        op_copy(c).start()
    for c in range(comps):
        packf[pl.ds(c * nodes, nodes), :] = mv[c]
    packed[...] = packf[...].astype(BF16)
    head = packed[:, :LANES]
    tail = packed[:, nboxes - LANES:]
    picked = dot_nt(jnp.concatenate([low_pick, chooser], axis=0), head)
    face_out[0] = picked[:FACE].astype(BF16)
    face_out[1] = dot_nt(high_pick, tail).astype(BF16)
    for p in range(owners):
        ghost_out[p] = picked[FACE + p * cap:FACE + (p + 1) * cap].astype(BF16)

    barrier_count = owners - 1 + jnp.where(leaf > 0, 1, 0) + jnp.where(leaf < groups - 1, 1, 0)
    pl.semaphore_wait(barrier, barrier_count)

    def face_copy(side):
        step = -1 if side == 0 else 1
        return pltpu.make_async_remote_copy(
            src_ref=face_out.at[side], dst_ref=face_in.at[1 - side],
            send_sem=face_send.at[side], recv_sem=face_recv.at[1 - side],
            device_id=(leaf + step, me), device_id_type=MESH,
        )

    def ghost_copy(k):
        peer = lax.rem(me + k, owners)
        return pltpu.make_async_remote_copy(
            src_ref=ghost_out.at[peer], dst_ref=ghost_in.at[me],
            send_sem=ghost_send.at[k], recv_sem=ghost_recv.at[k],
            device_id=(leaf, peer), device_id_type=MESH,
        )

    @pl.when(leaf > 0)
    def _():
        face_copy(0).start()

    @pl.when(leaf < groups - 1)
    def _():
        face_copy(1).start()

    lax.fori_loop(1, owners, lambda k, carry: (ghost_copy(k).start(), carry)[1], 0)

    def translate(c, weights, y, z):
        lhs = opv[c].reshape(span * dirs, width)
        product = jnp.dot(lhs, weights, preferred_element_type=F32)
        for t in range(y.shape[0]):
            y[t] = product[:, t * LANES:(t + 1) * LANES]
        for d in range(dirs):
            for t in range(y.shape[0]):
                at = (d * y.shape[0] + t) * LANES
                z[c, :span, at:at + LANES] = y[t, pl.ds(d, span, stride=dirs), :].astype(BF16)

    held = za.shape[1]

    def gather(z, select):
        rows = z[...].reshape(comps * held, z.shape[2])
        return jnp.dot(rows, select[...], preferred_element_type=F32)

    def first_pass(c, carry):
        op_copy(c).wait()
        translate(c, packed[:, :first], y_first, za)
        return carry

    lax.fori_loop(0, comps, first_pass, 0)
    gathered = gather(za, ga)
    for c in range(comps):
        out[c] = gathered[c * held:c * held + nodes]

    @pl.when(leaf < groups - 1)
    def _():
        face_copy(1).wait_send()
        face_copy(0).wait_recv()

    @pl.when(leaf > 0)
    def _():
        face_copy(0).wait_send()
        face_copy(1).wait_recv()

    lax.fori_loop(1, owners, lambda k, carry: (ghost_copy(k).wait(), carry)[1], 0)

    arrived = [face_in[0].astype(F32), face_in[1].astype(F32)]
    ghosts = [ghost_in[p].astype(F32) for p in range(owners)]
    arrived = jnp.concatenate(arrived + ghosts, axis=0)
    pad = pb.shape[1] - rest - arrived.shape[0]
    if pad:
        arrived = jnp.concatenate([arrived, jnp.zeros((pad, width), F32)], axis=0)
    pb[:, :rest] = packed[:, first:]
    pb[:, rest:] = arrived.T.astype(BF16)

    def second_pass(c, carry):
        translate(c, pb[...], y_rest, zb)
        return carry

    lax.fori_loop(0, comps, second_pass, 0)

    gathered = gather(zb, gb)
    for c in range(comps):
        out[c] = out[c] + gathered[c * held:c * held + nodes]


def local(groups, owners, multipoles, operators, lists, send_slots):
    comps, nodes, nboxes = multipoles.shape
    dirs, width, _ = operators.shape
    cap = send_slots.shape[2]
    first = nboxes // 256 * 256 if nboxes % 256 else nboxes - 256
    extra = round_up(nboxes - first + 2 * FACE + owners * cap, LANES)
    extra = max(extra, 256)
    span = round_up(nodes, 8)
    anywhere = pl.BlockSpec(memory_space=pl.ANY)
    vmem = pl.BlockSpec(memory_space=pltpu.VMEM)
    dma = pltpu.SemaphoreType.DMA
    return pl.pallas_call(
        functools.partial(kernel, groups, owners, cap, first),
        out_shape=pltpu.VMEM((comps, nodes, nboxes), F32),
        in_specs=[anywhere, anywhere, vmem, vmem],
        out_specs=vmem,
        scratch_shapes=[
            pltpu.VMEM((comps, span, dirs, width), BF16),
            pltpu.VMEM((comps, nodes, nboxes), F32),
            pltpu.VMEM((width, nboxes), F32),
            pltpu.VMEM((width, nboxes), BF16),
            pltpu.VMEM((width, extra), BF16),
            pltpu.VMEM((first // LANES, span * dirs, LANES), F32),
            pltpu.VMEM((extra // LANES, span * dirs, LANES), F32),
            pltpu.VMEM((comps, round_up(nodes, 16), dirs * first), BF16),
            pltpu.VMEM((comps, round_up(nodes, 16), dirs * extra), BF16),
            pltpu.VMEM((dirs * first, nboxes), BF16),
            pltpu.VMEM((dirs * extra, nboxes), BF16),
            pltpu.VMEM((2, FACE, width), BF16),
            pltpu.VMEM((2, FACE, width), BF16),
            pltpu.VMEM((owners, cap, width), BF16),
            pltpu.VMEM((owners, cap, width), BF16),
            dma((comps,)), dma, dma((2,)), dma((2,)), dma((owners,)), dma((owners,)),
        ],
        compiler_params=pltpu.CompilerParams(
            collective_id=0, has_side_effects=True, vmem_limit_bytes=58 << 20
        ),
        cost_estimate=pl.CostEstimate(
            flops=2 * dirs * width * width * nboxes,
            bytes_accessed=2 * dirs * width * width + 8 * width * nboxes,
            transcendentals=0,
        ),
    )(
        multipoles,
        operators.transpose(1, 0, 2),
        lists.T,
        send_slots.reshape(owners, cap).T,
    )


def solution(mesh):
    return jax.shard_map(
        functools.partial(local, mesh.shape["leaf"], mesh.shape["owner"]),
        mesh=mesh,
        in_specs=(
            P(None, None, ("leaf", "owner")),
            P(),
            P(("leaf", "owner"), None),
            P(("leaf", "owner"), None, None),
        ),
        out_specs=P(None, None, ("leaf", "owner")),
        check_vma=False,
    )
```
